256 devices in a mesh: group: 8 (over z_hi, core), gx: 4 (over x), gy: 8 (over y, z_lo).
Axes of the slice: x: 4, y: 4, z: 8 (z_hi: 4, z_lo: 2; z = z_hi * 2 + z_lo), core: 2. Of those that a mesh axis runs over, the one named last changes fastest.
Arguments:
- start_vectors: float32 [8, 4, 8, 8, 384, 128], P('group', 'gx', 'gy')
- tile_blocks: bfloat16 [8, 4, 8, 8, 4, 384, 384], P('group', 'gx', 'gy')
- block_columns: int32 [8, 4, 8, 8, 4], P('group', 'gx', 'gy'), may hold values from 0 to 11, as said below
- sleeve_rod: int32 [4, 8, 7, 8, 8], P('gx', 'gy'), may hold values from -1 to 511, as said below
- sleeve_membrane: int32 [4, 8, 7, 8, 8], P('gx', None, None, 'gy'), may hold values from -1 to 511, as said below
- sleeve_stiffness: float32 [4, 8, 7, 8, 8], P('gx', None, None, 'gy'), may hold values from 0.25 to 4
Outputs:
- final_vectors: float32 [8, 4, 8, 8, 384, 128], P('group', 'gx', 'gy')
- norms: float32 [3, 128], replicated
The draws below stay inside these ranges and needn't reach their ends.
Inputs may be any that keep to these rules, and one draw needn't show every extreme that they name: `block_columns`: entry 0 of block row r is r itself; every other entry names one of the device's 8 blocks, or 8 to 11 for the west, east, south and north ghost blocks. sleeve_rod[x, y, m, y2, :] lists the nodes of rod device (0, x, y) tied to membrane tile (m + 1, x, y2); -1 marks an empty slot and live slots come first. In every draw one membrane tile receives 8 live slots from each of the 8 rod devices of its column. `sleeve_membrane`: -1 at exactly the slots where sleeve_rod is -1; elsewhere a node of membrane tile (m + 1, x, y2).
All inputs are finite; a program needn't handle non-finite values.
Results may differ from the reference program's by a relative error of at most 0.005.
Values may be sent and summed in bfloat16 or wider, within the bound.
No kernel may reach another device: no remote copies, remote signals or barrier semaphores. Data moves between devices by JAX's collectives and lax.ppermute only.
A program may use at most 64 MiB of HBM per device.

```python
import math
import jax
import jax.numpy as jnp
from jax import lax

TILE = 384
NB = 8
KB = 4
S = 128
CAP = 8
MATVECS = 3
MEMB = 7
NODES_DEV = 512
N_GROUP = 8
N_GX = 4
N_GY = 8


def device_ramp():
    position = (jnp.arange(N_GROUP)[:, None, None] * N_GX + jnp.arange(N_GX)[None, :, None]) * N_GY + jnp.arange(N_GY)[None, None, :]
    return jnp.exp(math.log(3.0) * position.astype(jnp.float32) / max(N_GROUP * N_GX * N_GY - 1, 1))


def draw_start_vectors(key, part):
    first, second = jax.random.split(jax.random.fold_in(key, 3))
    shape = (N_GROUP, N_GX, N_GY, NB, TILE, S)
    noise = jax.random.normal(first, shape, jnp.float32)
    column = jnp.exp(jax.random.uniform(second, (S,), jnp.float32, math.log(0.3), math.log(3.0)))
    return noise * column * device_ramp()[:, :, :, None, None, None]


def draw_tile_blocks(key, part):
    first, second = jax.random.split(jax.random.fold_in(key, 13))
    shape = (N_GROUP, N_GX, N_GY, NB, KB, TILE, TILE)
    noise = jax.random.normal(first, shape, jnp.float32)
    row_scale = jnp.exp(jax.random.uniform(second, (N_GROUP, N_GX, N_GY, NB, 1, TILE, 1), jnp.float32, math.log(0.4), math.log(4.0)))
    ramp = device_ramp()[:, :, :, None, None, None, None]
    return (noise * row_scale * ramp / math.sqrt(KB * TILE)).astype(jnp.bfloat16)


def draw_block_columns(key, part):
    shape = (N_GROUP, N_GX, N_GY, NB, KB)
    extra = jax.random.randint(jax.random.fold_in(key, 11), shape, 0, NB + 4, dtype=jnp.int32)
    own_row = jnp.broadcast_to(jnp.arange(NB, dtype=jnp.int32)[:, None], (NB, KB))
    slot_first = jnp.arange(KB)[None, :] == 0
    return jnp.where(slot_first, own_row, extra).astype(jnp.int32)


def sleeve_lists(key):
    keys = jax.random.split(jax.random.fold_in(key, 29), 8)
    shape = (N_GX, N_GY, MEMB, N_GY)
    base = jax.random.randint(keys[0], shape, 1, max(CAP // 4, 1) + 1, dtype=jnp.int32)
    hot_rows = jax.random.randint(keys[1], (N_GX, N_GY, 1, 1), 0, 4, dtype=jnp.int32) == 0
    heavy = jax.random.randint(keys[2], shape, max(CAP // 2, 1), CAP + 1, dtype=jnp.int32)
    counts = jnp.where(hot_rows, heavy, base)
    full_x = jax.random.randint(keys[3], (), 0, N_GX, dtype=jnp.int32)
    full_m = jax.random.randint(keys[4], (), 0, MEMB, dtype=jnp.int32)
    full_y = jax.random.randint(keys[5], (), 0, N_GY, dtype=jnp.int32)
    forced = (jnp.arange(N_GX)[:, None, None, None] == full_x) & (jnp.arange(MEMB)[None, None, :, None] == full_m) & (jnp.arange(N_GY)[None, None, None, :] == full_y)
    counts = jnp.where(forced, CAP, counts)
    live = jnp.arange(CAP)[None, None, None, None, :] < counts[..., None]
    rod_nodes = jax.random.randint(keys[6], shape + (CAP,), 0, NODES_DEV, dtype=jnp.int32)
    memb_nodes = jax.random.randint(keys[7], shape + (CAP,), 0, NODES_DEV, dtype=jnp.int32)
    return (jnp.where(live, rod_nodes, -1).astype(jnp.int32), jnp.where(live, memb_nodes, -1).astype(jnp.int32))


def draw_sleeve_rod(key, part):
    return sleeve_lists(key)[0]


def draw_sleeve_membrane(key, part):
    return sleeve_lists(key)[1]


def levels(key, shape, cuts, smallest, top_value):
    def one(dim, parts):
        draws = jax.random.uniform(jax.random.fold_in(jax.random.fold_in(key, 6), dim), (parts,), jnp.float32, smallest / len(cuts), top_value / len(cuts))
        return jnp.repeat(jnp.exp(draws), shape[dim] // parts).reshape((-1,) + (1,) * (len(shape) - dim - 1))

    gain = one(*cuts[0])
    for cut in cuts[1:]:
        gain = gain * one(*cut)
    return gain


def setup_inputs(seed: int = 0) -> dict:
    arg_keys = jax.random.split(jax.random.key(seed), 7)
    start_vectors = draw_start_vectors(jax.random.fold_in(arg_keys[6], 71), 0)
    tile_blocks = draw_tile_blocks(jax.random.fold_in(arg_keys[6], 71), 0)
    block_columns = draw_block_columns(jax.random.fold_in(arg_keys[6], 71), 0)
    sleeve_rod = draw_sleeve_rod(jax.random.fold_in(arg_keys[6], 71), 0)
    sleeve_membrane = draw_sleeve_membrane(jax.random.fold_in(arg_keys[6], 71), 0)
    sleeve_stiffness = jnp.clip(jnp.exp(math.log(4.0) - 2.7725887 * jax.random.uniform(arg_keys[5], (N_GX, N_GY, MEMB, N_GY, CAP), jnp.float32) ** levels(arg_keys[5], (N_GX, N_GY, MEMB, N_GY, CAP), ((0, 4), (3, 8)), -0.2, 0.2)), 0.25, 4.0)
    return dict(start_vectors=start_vectors, tile_blocks=tile_blocks, block_columns=block_columns, sleeve_rod=sleeve_rod, sleeve_membrane=sleeve_membrane, sleeve_stiffness=sleeve_stiffness)


def reference(start_vectors, tile_blocks, block_columns, sleeve_rod, sleeve_membrane, sleeve_stiffness):
    devices_all = N_GROUP * N_GX * N_GY
    nodes = NB * TILE // 6
    payload = 6 * S
    blocks = tile_blocks.reshape(devices_all, NB, KB, TILE, TILE)
    columns = block_columns.reshape(devices_all, NB * KB)
    live = sleeve_rod >= 0
    rod_safe = jnp.maximum(sleeve_rod, 0)
    memb_safe = jnp.maximum(sleeve_membrane, 0)
    stiffs = jnp.where(live, sleeve_stiffness, jnp.float32(0.0))
    shape5 = sleeve_rod.shape
    x_index = jnp.broadcast_to(jnp.arange(N_GX, dtype=jnp.int32)[:, None, None, None, None], shape5)
    y_source = jnp.broadcast_to(jnp.arange(N_GY, dtype=jnp.int32)[None, :, None, None, None], shape5)
    m_index = jnp.broadcast_to(jnp.arange(MEMB, dtype=jnp.int32)[None, None, :, None, None], shape5) + 1
    y_target = jnp.broadcast_to(jnp.arange(N_GY, dtype=jnp.int32)[None, None, None, :, None], shape5)
    g_zero = jnp.zeros(shape5, jnp.int32)

    def one_device(args):
        local_blocks, local_ext, local_cols = args
        picked = jnp.take(local_ext, local_cols, axis=0).reshape(NB, KB, TILE, S)
        return jnp.einsum('rkij,rkjs->ris', local_blocks.astype(jnp.float32), picked.astype(jnp.float32), precision=lax.Precision.HIGHEST)
    current = start_vectors
    norms = []
    for matvec in range(MATVECS):
        rounded = current.astype(jnp.bfloat16)
        zero_x = jnp.zeros_like(rounded[:, :1, :, 0])
        west = jnp.concatenate([zero_x, rounded[:, :-1, :, NB - 1]], axis=1)
        east = jnp.concatenate([rounded[:, 1:, :, 0], zero_x], axis=1)
        zero_y = jnp.zeros_like(rounded[:, :, :1, 0])
        south = jnp.concatenate([zero_y, rounded[:, :, :-1, 1]], axis=2)
        north = jnp.concatenate([rounded[:, :, 1:, NB - 2], zero_y], axis=2)
        extended = jnp.concatenate([rounded, west[:, :, :, None], east[:, :, :, None], south[:, :, :, None], north[:, :, :, None]], axis=3)
        extended = extended.reshape(devices_all, NB + 4, TILE, S)
        product = lax.map(one_device, (blocks, extended, columns)).reshape(N_GROUP, N_GX, N_GY, NB, TILE, S)
        node_rows = rounded.reshape(N_GROUP, N_GX, N_GY, nodes, payload).astype(jnp.float32)
        rod_values = node_rows[0][x_index, y_source, rod_safe]
        memb_values = node_rows[m_index, x_index, y_target, memb_safe]
        delta = stiffs[..., None] * (memb_values - rod_values)
        reaction = delta.astype(jnp.bfloat16).astype(jnp.float32)
        coupling = jnp.zeros_like(node_rows).at[m_index, x_index, y_target, memb_safe].add(delta)
        coupling = coupling.at[g_zero, x_index, y_source, rod_safe].add(-reaction)
        coupled = product + coupling.reshape(product.shape)
        squares = lax.optimization_barrier(jnp.sum(coupled * coupled, axis=(0, 1, 2, 3, 4)))
        scale = jnp.sqrt(squares / (devices_all * NB * TILE) + 1e-06)
        current = coupled / scale
        norms.append(scale)
    return (current, jnp.stack(norms))
```

```python
import functools

import jax
import jax.numpy as jnp
from jax import lax
from jax.experimental import pallas as pl
from jax.experimental.pallas import tpu as pltpu
from jax.sharding import Mesh, PartitionSpec as P

MATVECS = 3
TILE = 384
NB = 8
KB = 4
S = 128
CAP = 8
DOFS = 6
NODES = NB * TILE // DOFS
ROWS = NB * TILE
GY_N = 8
PAIRS = 4
SLOTS = 7 * GY_N * CAP
MSLOTS = GY_N * CAP
ROWS_MSG = DOFS * CAP
EPS = 1e-06
ALL_DOFS = 8 * 4 * 8 * ROWS

GROUP = ("zh", "core")
GY = ("y", "zl")
EVERY = ("zh", "core", "gx", "y", "zl")
ORDER = (0, 1, 3, 5, 2, 4, 6)

VMEM = pl.BlockSpec(memory_space=pltpu.VMEM)
SMEM = pl.BlockSpec(memory_space=pltpu.SMEM)
BF16 = jnp.bfloat16
F32 = jnp.float32


def dot(a, b):
    return jnp.dot(a, b, preferred_element_type=F32)


def update_kernel(first, last, *refs):
    refs = list(refs)
    take = lambda n: [refs.pop(0) for _ in range(n)]
    (rod, base) = take(2)
    if not first:
        (inv, recv_a, recv_b, own_a, own_b, kappa, scatter) = take(7)
    if not last:
        (gather,) = take(1)
        (rounded, east, west, north, south, send_a, send_b) = take(7)
    else:
        (y,) = take(1)
    if not first:
        (squares,) = take(1)
    (slots,) = take(1)
    if not last:
        (y,) = take(1)
    is_rod = rod[0] == 1

    if not first:
        own = [own_b.at[0], own_a.at[1], own_a.at[2], own_a.at[3], own_b.at[1], own_b.at[2], own_b.at[3]]
        other = [recv_a.at[0], recv_a.at[1], recv_a.at[2], recv_a.at[3], recv_b.at[0], recv_b.at[1], recv_b.at[2]]

        def difference(q, mine, theirs):
            gap = mine[...].astype(F32) - theirs[...].astype(F32)
            stiff = kappa[q * MSLOTS : (q + 1) * MSLOTS].reshape(GY_N, 1, CAP, S)
            slots[q * GY_N : (q + 1) * GY_N] = gap.reshape(GY_N, DOFS, CAP, S) * stiff

        @pl.when(is_rod)
        def _():
            for q in range(7):
                difference(q, own[q], other[q])

        @pl.when(jnp.logical_not(is_rod))
        def _():
            difference(0, own_a.at[0], recv_a.at[0])
            slots[GY_N : 2 * GY_N] = jnp.zeros((GY_N, DOFS, CAP, S), F32)

        scale = inv[...]

        def finish(d, coupling):
            value = (base[pl.ds(d, NODES, stride=DOFS), :] + coupling) * scale
            y[pl.ds(d, NODES, stride=DOFS), :] = value
            part = jnp.sum(jnp.square(value).reshape(NODES // 8, 8, S), axis=0)
            return jnp.sum(part, axis=0, keepdims=True)

        @pl.when(is_rod)
        def _():
            total = jnp.zeros((1, S), F32)
            for d in range(DOFS):
                delta = slots[:, d].reshape(SLOTS, S)
                total += finish(d, dot(scatter[...], delta.astype(BF16)))
            squares[...] = total

        @pl.when(jnp.logical_not(is_rod))
        def _():
            total = jnp.zeros((1, S), F32)
            place = scatter[:, : 2 * MSLOTS]
            for d in range(DOFS):
                delta = slots[: 2 * GY_N, d].reshape(2 * MSLOTS, S)
                high = delta.astype(BF16)
                low = (delta - high.astype(F32)).astype(BF16)
                total += finish(d, dot(place, high) + dot(place, low))
            squares[...] = total

    if not last:
        source = base if first else y
        for r in range(NB):
            rounded[r] = source[r * TILE : (r + 1) * TILE].astype(BF16)
        east[...] = rounded[NB - 1]
        west[...] = rounded[0]
        north[...] = rounded[1]
        south[...] = rounded[NB - 2]

        def collect(count):
            pick = gather[: count * MSLOTS]
            for d in range(DOFS):
                values = source[pl.ds(d, NODES, stride=DOFS), :].astype(BF16)
                rows = dot(pick, values)
                slots[: count * GY_N, d] = rows.reshape(count * GY_N, CAP, S)

        def message(q):
            return slots[q * GY_N : (q + 1) * GY_N].reshape(GY_N, ROWS_MSG, S).astype(BF16)

        @pl.when(is_rod)
        def _():
            collect(7)
            send_a[0] = jnp.zeros((GY_N, ROWS_MSG, S), BF16)
            send_b[0] = message(0)
            for q in range(3):
                send_a[q + 1] = message(q + 1)
                send_b[q + 1] = message(q + 4)

        @pl.when(jnp.logical_not(is_rod))
        def _():
            collect(1)
            send_a[0] = message(0)
            send_b[0] = message(0)
            for q in range(1, PAIRS):
                send_a[q] = jnp.zeros((GY_N, ROWS_MSG, S), BF16)
                send_b[q] = jnp.zeros((GY_N, ROWS_MSG, S), BF16)


def update(first, last, args):
    out = []
    if not last:
        out += [jax.ShapeDtypeStruct((NB, TILE, S), BF16)]
        out += [jax.ShapeDtypeStruct((TILE, S), BF16)] * 4
        out += [jax.ShapeDtypeStruct((PAIRS, GY_N, ROWS_MSG, S), BF16)] * 2
    else:
        out += [jax.ShapeDtypeStruct((ROWS, S), F32)]
    if not first:
        out += [jax.ShapeDtypeStruct((1, S), F32)]
    scratch = [pltpu.VMEM((7 * GY_N, DOFS, CAP, S), F32)]
    if not last:
        scratch += [pltpu.VMEM((ROWS, S), F32)]
    return pl.pallas_call(
        functools.partial(update_kernel, first, last),
        out_shape=out,
        in_specs=[SMEM] + [VMEM] * (len(args) - 1),
        out_specs=[VMEM] * len(out),
        scratch_shapes=scratch,
        compiler_params=pltpu.CompilerParams(vmem_limit_bytes=32 * 1024 * 1024),
        name="update",
    )(*args)


def product_kernel(columns, blocks, rounded, west, east, south, north, out, extended):
    r = pl.program_id(0)

    @pl.when(r == 0)
    def _():
        extended[:NB] = rounded[...]
        extended[NB] = west[...]
        extended[NB + 1] = east[...]
        extended[NB + 2] = south[...]
        extended[NB + 3] = north[...]

    total = dot(blocks[0, 0], extended[columns[r, 0]])
    for k in range(1, KB):
        total += dot(blocks[0, k], extended[columns[r, k]])
    out[...] = total


def product(columns, blocks, rounded, west, east, south, north):
    return pl.pallas_call(
        product_kernel,
        out_shape=jax.ShapeDtypeStruct((ROWS, S), F32),
        grid=(NB,),
        in_specs=[
            SMEM,
            pl.BlockSpec((1, KB, TILE, TILE), lambda r: (r, 0, 0, 0)),
            VMEM,
            VMEM,
            VMEM,
            VMEM,
            VMEM,
        ],
        out_specs=pl.BlockSpec((TILE, S), lambda r: (r, 0)),
        scratch_shapes=[pltpu.VMEM((NB + 4, TILE, S), BF16)],
        compiler_params=pltpu.CompilerParams(vmem_limit_bytes=32 * 1024 * 1024),
        cost_estimate=pl.CostEstimate(
            flops=2 * NB * KB * TILE * TILE * S, bytes_accessed=12_000_000, transcendentals=0
        ),
        name="product",
    )(columns, blocks, rounded, west, east, south, north)


def chain(count, step):
    return [(i, i + step) for i in range(count) if 0 <= i + step < count]


def halos(rounded_edges):
    (last, head, second, sixth) = rounded_edges
    west = lax.ppermute(last, "gx", chain(4, 1))
    east = lax.ppermute(head, "gx", chain(4, -1))
    south = lax.ppermute(second, GY, chain(8, 1))
    north = lax.ppermute(sixth, GY, chain(8, -1))
    return (west, east, south, north)


def norm_of(squares):
    spread = jnp.broadcast_to(squares, (256, S))
    gathered = lax.all_to_all(spread, EVERY, split_axis=0, concat_axis=0, tiled=True)
    return jnp.sqrt(jnp.sum(gathered, axis=0, keepdims=True) / ALL_DOFS + EPS)


def exchange(group, send_a, send_b):
    passed = lax.ppermute(send_b, GROUP, [(0, 1), (1, 0)])
    block = jnp.arange(PAIRS)
    relay = (group == 1) | ((group == 0) & (block == 0))
    send = jnp.where(relay[:, None, None, None], passed, send_a)
    received = lax.all_to_all(
        send.reshape(PAIRS * GY_N, ROWS_MSG, S),
        ("zh", "y", "zl"),
        split_axis=0,
        concat_axis=0,
        tiled=True,
    ).reshape(PAIRS, GY_N, ROWS_MSG, S)
    handed = lax.ppermute(received[1:], GROUP, [(1, 0)])
    return (received, handed)


def local(start_vectors, tile_blocks, block_columns, sleeve_rod, sleeve_membrane, sleeve_stiffness):
    group = lax.axis_index(GROUP)
    is_rod = group == 0
    memb = jnp.maximum(group - 1, 0)
    order = jnp.array(ORDER, jnp.int32)
    blocks = tile_blocks[0, 0, 0]
    columns = block_columns[0, 0, 0]

    rod_nodes = jnp.take(sleeve_rod[0, 0], order, axis=0).reshape(SLOTS)
    memb_nodes = lax.dynamic_index_in_dim(
        sleeve_membrane[0, :, :, 0, :], memb, axis=1, keepdims=False
    ).reshape(MSLOTS)
    memb_nodes = jnp.concatenate([memb_nodes, jnp.full((SLOTS - MSLOTS,), -1, jnp.int32)])
    nodes = jnp.where(is_rod, rod_nodes, memb_nodes)
    ids = jnp.arange(NODES, dtype=jnp.int32)
    gather = (nodes[:, None] == ids[None, :]).astype(BF16)
    scatter = (ids[:, None] == nodes[None, :]).astype(BF16)
    rod_flag = is_rod.astype(jnp.int32).reshape(1)

    start = start_vectors[0, 0, 0].reshape(ROWS, S)
    state = update(True, False, [rod_flag, start, gather])

    stiff = sleeve_stiffness[0, :, :, 0, :]
    rod_stiff = lax.all_to_all(
        stiff.reshape(GY_N, 7 * CAP), GY, split_axis=0, concat_axis=0, tiled=True
    ).reshape(GY_N, 7, CAP)
    rod_stiff = jnp.take(rod_stiff, order, axis=1).transpose(1, 0, 2).reshape(SLOTS)
    memb_stiff = lax.dynamic_index_in_dim(stiff, memb, axis=1, keepdims=False).reshape(MSLOTS)
    memb_stiff = jnp.concatenate([memb_stiff, jnp.zeros((SLOTS - MSLOTS,), F32)])
    kappa = jnp.where(is_rod, rod_stiff, memb_stiff)
    kappa = jnp.broadcast_to(kappa[:, None], (SLOTS, S))

    scales = []
    inverse = jnp.ones((1, S), F32)
    for turn in range(MATVECS):
        last = turn == MATVECS - 1
        (rounded, *edges) = state[:5]
        (send_a, send_b) = state[5:7]
        (recv_a, recv_b) = exchange(group, send_a, send_b)
        if turn:
            scales.append(norm_of(state[7]))
            inverse = 1.0 / scales[-1]
        base = product(columns, blocks, rounded, *halos(edges))
        args = [rod_flag, base, inverse, recv_a, recv_b, send_a, send_b, kappa, scatter]
        state = update(False, last, args + ([] if last else [gather]))
    (value, squares) = state
    scales.append(norm_of(squares))
    final = (value / scales[-1]).reshape(1, 1, 1, NB, TILE, S)
    return (final, jnp.concatenate(scales, axis=0))


def solution(mesh):
    fine = Mesh(mesh.devices.reshape(4, 2, 4, 4, 2), EVERY)
    spread = (GROUP, "gx", GY)
    return jax.shard_map(
        local,
        mesh=fine,
        in_specs=(
            P(*spread, None, None, None),
            P(*spread, None, None, None, None),
            P(*spread, None, None),
            P("gx", GY, None, None, None),
            P("gx", None, None, GY, None),
            P("gx", None, None, GY, None),
        ),
        out_specs=(P(*spread, None, None, None), P()),
        check_vma=False,
    )
```

```python
import functools

import jax
import jax.numpy as jnp
from jax import lax
from jax.experimental import pallas as pl
from jax.experimental.pallas import tpu as pltpu
from jax.sharding import PartitionSpec as P

MATVECS = 3
TILE = 384
NB = 8
KB = 4
S = 128
CAP = 8
DOFS = 6
NODES = NB * TILE // DOFS
ROWS = NB * TILE
GROUPS = 8
MEMB = GROUPS - 1
GX_N = 4
GY_N = 8
DEVICES = GROUPS * GX_N * GY_N
SLOTS = MEMB * GY_N * CAP
MSLOTS = GY_N * CAP
MESSAGE = DOFS * CAP
EPS = 1e-06
ALL_DOFS = DEVICES * ROWS
LOWEST, HIGHEST = 1e-20, 1e20

EVERY = ("group", "gx", "gy")

VMEM = pl.BlockSpec(memory_space=pltpu.VMEM)
SMEM = pl.BlockSpec(memory_space=pltpu.SMEM)
BF16 = jnp.bfloat16
F32 = jnp.float32


def dot(a, b):
    return jnp.dot(a, b, preferred_element_type=F32)


def update_kernel(turn, scaled, *refs):
    refs = list(refs)
    take = lambda n: [refs.pop(0) for _ in range(n)]
    first, last = turn == 0, turn == MATVECS
    (rod, base) = take(2)
    if first:
        (stiff_message, gather) = take(2)
    else:
        (received, own, kappa_in, scatter) = take(4)
        if not last:
            (gather,) = take(1)
        if scaled:
            (inverse,) = take(1)
    if last:
        (y,) = take(1)
    else:
        (rounded, east, west, north, south, send) = take(6)
    if not first:
        (squares,) = take(1)
    kappa = None
    if turn == 1:
        (kappa,) = take(1)
    elif not first:
        kappa = kappa_in
    (slots,) = take(1)
    if not first and not last:
        (y,) = take(1)
    is_rod = rod[0] == 1

    def on_rod(f):
        pl.when(is_rod)(f)

    def on_membrane(f):
        pl.when(jnp.logical_not(is_rod))(f)

    if not first:

        def difference(q, block):
            gap = own[block].astype(F32) - received[block].astype(F32)
            stiff = kappa[q * MSLOTS : (q + 1) * MSLOTS].reshape(GY_N, 1, CAP, S)
            slots[q * GY_N : (q + 1) * GY_N] = gap.reshape(GY_N, DOFS, CAP, S) * stiff

        @on_rod
        def _():
            if turn == 1:
                parts = received[0].astype(F32)
                lane = lax.broadcasted_iota(jnp.int32, parts.shape, 2)
                low = jnp.sum(jnp.where(lane < 3, parts, 0.0), axis=2, keepdims=True)
                high = jnp.sum(
                    jnp.where((lane >= 3) & (lane < 6), parts, 0.0)[:, :CAP], axis=2, keepdims=True
                )
                for m in range(MEMB):
                    value = low[:, m * CAP : (m + 1) * CAP] if m < DOFS else high
                    kappa[m * MSLOTS : (m + 1) * MSLOTS] = jnp.broadcast_to(
                        value, (GY_N, CAP, S)
                    ).reshape(MSLOTS, S)
            for q in range(MEMB):
                difference(q, q + 1)

        @on_membrane
        def _():
            if turn == 1:
                kappa[...] = kappa_in[...]
            difference(0, 0)
            slots[GY_N : 2 * GY_N] = jnp.zeros((GY_N, DOFS, CAP, S), F32)

        def finish(d, coupling):
            value = base[pl.ds(d, NODES, stride=DOFS), :] + coupling
            if scaled:
                value = value * inverse[...]
            y[pl.ds(d, NODES, stride=DOFS), :] = value
            part = jnp.sum(jnp.square(value).reshape(NODES // 8, 8, S), axis=0)
            return jnp.sum(part, axis=0, keepdims=True)

        @on_rod
        def _():
            total = jnp.zeros((1, S), F32)
            for d in range(DOFS):
                delta = slots[:, d].reshape(SLOTS, S)
                total += finish(d, dot(scatter[...], delta.astype(BF16)))
            squares[...] = total

        @on_membrane
        def _():
            total = jnp.zeros((1, S), F32)
            place = scatter[:, : 2 * MSLOTS]
            for d in range(DOFS):
                delta = slots[: 2 * GY_N, d].reshape(2 * MSLOTS, S)
                high = delta.astype(BF16)
                low = (delta - high.astype(F32)).astype(BF16)
                total += finish(d, dot(place, high) + dot(place, low))
            squares[...] = total

    if not last:
        source = base if first else y

        def collect(count):
            pick = gather[: count * MSLOTS]
            for d in range(DOFS):
                values = source[pl.ds(d, NODES, stride=DOFS), :].astype(BF16)
                rows = dot(pick, values)
                slots[: count * GY_N, d] = rows.reshape(count * GY_N, CAP, S)

        def message(q):
            return slots[q * GY_N : (q + 1) * GY_N].reshape(GY_N, MESSAGE, S).astype(BF16)

        @on_rod
        def _():
            collect(MEMB)
            if first:
                send[0] = stiff_message[...]
            for q in range(MEMB):
                send[q + 1] = message(q)

        @on_membrane
        def _():
            collect(1)
            send[0] = message(0)

        for r in range(NB):
            rounded[r] = source[r * TILE : (r + 1) * TILE].astype(BF16)
        east[...] = rounded[NB - 1]
        west[...] = rounded[0]
        north[...] = rounded[1]
        south[...] = rounded[NB - 2]


def update(turn, scaled, args):
    first, last = turn == 0, turn == MATVECS
    if last:
        out = [jax.ShapeDtypeStruct((ROWS, S), F32)]
    else:
        out = [jax.ShapeDtypeStruct((NB, TILE, S), BF16)]
        out += [jax.ShapeDtypeStruct((TILE, S), BF16)] * 4
        out += [jax.ShapeDtypeStruct((GROUPS, GY_N, MESSAGE, S), BF16)]
    if not first:
        out += [jax.ShapeDtypeStruct((1, S), F32)]
    if turn == 1:
        out += [jax.ShapeDtypeStruct((SLOTS, S), F32)]
    scratch = [pltpu.VMEM((MEMB * GY_N, DOFS, CAP, S), F32)]
    if not first and not last:
        scratch += [pltpu.VMEM((ROWS, S), F32)]
    return pl.pallas_call(
        functools.partial(update_kernel, turn, scaled),
        out_shape=out,
        in_specs=[SMEM] + [VMEM] * (len(args) - 1),
        out_specs=[VMEM] * len(out),
        scratch_shapes=scratch,
        compiler_params=pltpu.CompilerParams(vmem_limit_bytes=32 * 1024 * 1024),
        name="update",
    )(*args)


def product_kernel(columns, blocks, rounded, west, east, south, north, out, extended):
    r = pl.program_id(0)

    @pl.when(r == 0)
    def _():
        extended[:NB] = rounded[...]
        extended[NB] = west[...]
        extended[NB + 1] = east[...]
        extended[NB + 2] = south[...]
        extended[NB + 3] = north[...]

    total = dot(blocks[0, 0], extended[columns[r, 0]])
    for k in range(1, KB):
        total += dot(blocks[0, k], extended[columns[r, k]])
    out[...] = total


def product(columns, blocks, rounded, west, east, south, north):
    return pl.pallas_call(
        product_kernel,
        out_shape=jax.ShapeDtypeStruct((ROWS, S), F32),
        grid=(NB,),
        in_specs=[
            SMEM,
            pl.BlockSpec((1, KB, TILE, TILE), lambda r: (r, 0, 0, 0)),
            VMEM,
            VMEM,
            VMEM,
            VMEM,
            VMEM,
        ],
        out_specs=pl.BlockSpec((TILE, S), lambda r: (r, 0)),
        scratch_shapes=[pltpu.VMEM((NB + 4, TILE, S), BF16)],
        compiler_params=pltpu.CompilerParams(vmem_limit_bytes=32 * 1024 * 1024),
        cost_estimate=pl.CostEstimate(
            flops=2 * NB * KB * TILE * TILE * S, bytes_accessed=12_000_000, transcendentals=0
        ),
        name="product",
    )(columns, blocks, rounded, west, east, south, north)


def chain(count, step):
    return [(i, i + step) for i in range(count) if 0 <= i + step < count]


def halos(edges):
    (last, head, second, sixth) = edges
    west = lax.ppermute(last, "gx", chain(GX_N, 1))
    east = lax.ppermute(head, "gx", chain(GX_N, -1))
    south = lax.ppermute(second, "gy", chain(GY_N, 1))
    north = lax.ppermute(sixth, "gy", chain(GY_N, -1))
    return (west, east, south, north)


def total_of(rows):
    count = rows.shape[0]
    spread = jnp.broadcast_to(rows.reshape(1, count * S), (DEVICES, count * S))
    gathered = lax.all_to_all(spread, EVERY, split_axis=0, concat_axis=0, tiled=True)
    return jnp.sum(gathered, axis=0).reshape(count, S)


def exchange(send):
    return lax.all_to_all(
        send.reshape(GROUPS * GY_N, MESSAGE, S),
        ("group", "gy"),
        split_axis=0,
        concat_axis=0,
        tiled=True,
    ).reshape(GROUPS, GY_N, MESSAGE, S)


def split(values):
    high = lax.reduce_precision(values, 8, 7)
    middle = lax.reduce_precision(values - high, 8, 7)
    return jnp.stack([high, middle, values - high - middle], axis=-1).astype(BF16)


def local(start_vectors, tile_blocks, block_columns, sleeve_rod, sleeve_membrane, sleeve_stiffness):
    group = lax.axis_index("group")
    is_rod = group == 0
    memb = jnp.maximum(group - 1, 0)
    blocks = tile_blocks[0, 0, 0]
    columns = block_columns[0, 0, 0]

    rod_nodes = sleeve_rod[0, 0].reshape(SLOTS)
    memb_nodes = lax.dynamic_index_in_dim(
        sleeve_membrane[0, :, :, 0, :], memb, axis=1, keepdims=False
    ).reshape(MSLOTS)
    rest = SLOTS - MSLOTS
    memb_nodes = jnp.concatenate([memb_nodes, jnp.full((rest,), -1, jnp.int32)])
    nodes = jnp.where(is_rod, rod_nodes, memb_nodes)
    ids = jnp.arange(NODES, dtype=jnp.int32)
    gather = (nodes[:, None] == ids[None, :]).astype(BF16)
    scatter = (ids[:, None] == nodes[None, :]).astype(BF16)
    rod_flag = is_rod.astype(jnp.int32).reshape(1)

    stiff = sleeve_stiffness[0, :, :, 0, :]
    pieces = split(stiff)
    low = pieces[:, :DOFS].reshape(GY_N, MESSAGE, 3)
    high = jnp.pad(pieces[:, DOFS], ((0, 0), (0, MESSAGE - CAP), (0, 0)))
    stiff_message = jnp.pad(jnp.concatenate([low, high], axis=2), ((0, 0), (0, 0), (0, S - 6)))
    kappa = lax.dynamic_index_in_dim(stiff, memb, axis=1, keepdims=False).reshape(MSLOTS)
    kappa = jnp.concatenate([kappa, jnp.zeros((rest,), F32)])
    kappa = jnp.broadcast_to(kappa[:, None], (SLOTS, S))

    def step(turn, state, kappa, inverse=None):
        (rounded, *edges, send) = state[:6]
        received = exchange(send)
        base = product(columns, blocks, rounded, *halos(edges))
        args = [rod_flag, base, received, send, kappa, scatter]
        if turn < MATVECS:
            args += [gather]
        if inverse is not None:
            args += [inverse]
        return update(turn, inverse is not None, args)

    start = start_vectors[0, 0, 0].reshape(ROWS, S)
    state = update(0, False, [rod_flag, start, stiff_message, gather])
    state = once = step(1, state, kappa)
    kappa = once[7]
    state = twice = step(2, state, kappa)
    (value, last) = step(3, state, kappa)

    sums = total_of(jnp.concatenate([once[6], twice[6], last], axis=0)) / ALL_DOFS
    safe = jnp.all((sums > LOWEST) & (sums < HIGHEST))
    first_norm = jnp.sqrt(sums[0:1] + EPS)

    def quick(_):
        second_norm = jnp.sqrt(sums[1:2] / jnp.square(first_norm) + EPS)
        both = first_norm * second_norm
        third_norm = jnp.sqrt(sums[2:3] / jnp.square(both) + EPS)
        final = value * (1.0 / (both * third_norm))
        return (final, jnp.concatenate([first_norm, second_norm, third_norm], axis=0))

    def careful(_):
        state = step(2, once, kappa, 1.0 / first_norm)
        second_norm = jnp.sqrt(total_of(state[6]) / ALL_DOFS + EPS)
        (value, squares) = step(3, state, kappa, 1.0 / second_norm)
        third_norm = jnp.sqrt(total_of(squares) / ALL_DOFS + EPS)
        norms = jnp.concatenate([first_norm, second_norm, third_norm], axis=0)
        return (value / third_norm, norms)

    (final, norms) = lax.cond(safe, quick, careful, None)
    return (final.reshape(1, 1, 1, NB, TILE, S), norms)


def solution(mesh):
    spread = ("group", "gx", "gy")
    return jax.shard_map(
        local,
        mesh=mesh,
        in_specs=(
            P(*spread, None, None, None),
            P(*spread, None, None, None, None),
            P(*spread, None, None),
            P("gx", "gy", None, None, None),
            P("gx", None, None, "gy", None),
            P("gx", None, None, "gy", None),
        ),
        out_specs=(P(*spread, None, None, None), P()),
        check_vma=False,
    )
```

```python
import functools

import jax
import jax.numpy as jnp
from jax import lax
from jax.experimental import pallas as pl
from jax.experimental.pallas import tpu as pltpu
from jax.sharding import Mesh, PartitionSpec as P

MATVECS = 3
TILE = 384
NB = 8
KB = 4
S = 128
CAP = 8
DOFS = 6
NODES = NB * TILE // DOFS
ROWS = NB * TILE
GROUPS = 8
MEMB = GROUPS - 1
GX_N = 4
GY_N = 8
DEVICES = GROUPS * GX_N * GY_N
SLOTS = MEMB * GY_N * CAP
MSLOTS = GY_N * CAP
MESSAGE = DOFS * CAP
EPS = 1e-06
ALL_DOFS = DEVICES * ROWS
LOWEST, HIGHEST = 1e-20, 1e20

GROUP = ("zh", "core")
GY = ("y", "zl")
AXES = ("zh", "core", "gx", "y", "zl")
PAIRS = GROUPS // 2

VMEM = pl.BlockSpec(memory_space=pltpu.VMEM)
SMEM = pl.BlockSpec(memory_space=pltpu.SMEM)
HBM = pl.BlockSpec(memory_space=pltpu.HBM)
BF16 = jnp.bfloat16
F32 = jnp.float32
VMEM_BYTES = 20 * 1024 * 1024


def dot(a, b):
    return jnp.dot(a, b, preferred_element_type=F32)


def update_kernel(turn, scaled, *refs):
    refs = list(refs)
    take = lambda n: [refs.pop(0) for _ in range(n)]
    first, last = turn == 0, turn == MATVECS
    (flags, base) = take(2)
    if first:
        (gather,) = take(1)
    else:
        (received, handed, own_a, own_b, kappa_in, scatter) = take(6)
        if not last:
            (gather,) = take(1)
        if turn == 1:
            (stiff_message,) = take(1)
        if scaled:
            (inverse,) = take(1)
    if last:
        (y,) = take(1)
    else:
        (rounded_out, x_even, x_odd, y_even, y_odd, send_b, own_a_out, own_b_out) = take(8)
    if not first:
        (squares,) = take(1)
    kappa = None
    if turn == 1:
        (kappa,) = take(1)
    elif not first:
        kappa = kappa_in
    (slots,) = take(1)
    if not last:
        (rounded, send_a, copied) = take(3)
    if not first and not last:
        (y,) = take(1)
    is_rod = flags[0] == 0

    def on_rod(f):
        pl.when(is_rod)(f)

    def on_membrane(f):
        pl.when(jnp.logical_not(is_rod))(f)

    if not first:

        def difference(q, mine, theirs):
            gap = mine[...].astype(F32) - theirs[...].astype(F32)
            stiff = kappa[q * MSLOTS : (q + 1) * MSLOTS].reshape(GY_N, 1, CAP, S)
            slots[q * GY_N : (q + 1) * GY_N] = gap.reshape(GY_N, DOFS, CAP, S) * stiff

        @on_rod
        def _():
            if turn == 1:
                parts = stiff_message[...].astype(F32)
                lane = lax.broadcasted_iota(jnp.int32, parts.shape, 2)
                low = jnp.sum(jnp.where(lane < 3, parts, 0.0), axis=2, keepdims=True)
                high = jnp.sum(
                    jnp.where((lane >= 3) & (lane < 6), parts, 0.0)[:, :CAP], axis=2, keepdims=True
                )
                for q in range(MEMB):
                    value = low[:, q * CAP : (q + 1) * CAP] if q < DOFS else high
                    kappa[q * MSLOTS : (q + 1) * MSLOTS] = jnp.broadcast_to(
                        value, (GY_N, CAP, S)
                    ).reshape(MSLOTS, S)
            difference(0, own_b.at[0], received.at[0])
            for q in range(1, PAIRS):
                difference(2 * q - 1, own_a.at[q], received.at[q])
                difference(2 * q, own_b.at[q], handed.at[q])

        @on_membrane
        def _():
            if turn == 1:
                kappa[...] = kappa_in[...]
            difference(0, own_a.at[0], received.at[0])
            slots[GY_N : 2 * GY_N] = jnp.zeros((GY_N, DOFS, CAP, S), F32)

        def pair_of(count, d):
            return jnp.concatenate(
                [slots[:count, d].reshape(count * CAP, S), slots[:count, d + 1].reshape(count * CAP, S)],
                axis=1,
            )

        def finish(d, coupling):
            value = base[pl.ds(d, NODES, stride=DOFS), :] + coupling
            if scaled:
                value = value * inverse[...]
            y[pl.ds(d, NODES, stride=DOFS), :] = value
            return jnp.sum(jnp.square(value).reshape(NODES // 8, 8, S), axis=0)

        @on_rod
        def _():
            total = jnp.zeros((8, S), F32)
            for d in range(0, DOFS, 2):
                coupling = dot(scatter[...], pair_of(MEMB * GY_N, d).astype(BF16))
                total += finish(d, coupling[:, :S]) + finish(d + 1, coupling[:, S:])
            squares[...] = jnp.sum(total, axis=0, keepdims=True)

        @on_membrane
        def _():
            total = jnp.zeros((8, S), F32)
            place = scatter[:, : 2 * MSLOTS]
            for d in range(0, DOFS, 2):
                delta = pair_of(2 * GY_N, d)
                high = delta.astype(BF16)
                low = (delta - high.astype(F32)).astype(BF16)
                coupling = dot(place, high) + dot(place, low)
                total += finish(d, coupling[:, :S]) + finish(d + 1, coupling[:, S:])
            squares[...] = jnp.sum(total, axis=0, keepdims=True)

    if not last:
        source = base if first else y

        for r in range(NB):
            rounded[r] = source[r * TILE : (r + 1) * TILE].astype(BF16)
        copies = [pltpu.make_async_copy(rounded, rounded_out, copied.at[0])]
        copies[0].start()
        odd_x, odd_y = flags[1], flags[2]
        x_even[...] = rounded[(NB - 1) * (1 - odd_x)]
        x_odd[...] = rounded[(NB - 1) * odd_x]
        y_even[...] = rounded[1 + (NB - 3) * odd_y]
        y_odd[...] = rounded[NB - 2 - (NB - 3) * odd_y]

        def collect(count):
            pick = gather[: count * MSLOTS]
            for d in range(0, DOFS, 2):
                values = jnp.concatenate(
                    [source[pl.ds(d + e, NODES, stride=DOFS), :].astype(BF16) for e in range(2)],
                    axis=1,
                )
                rows = dot(pick, values)
                for e in range(2):
                    slots[: count * GY_N, d + e] = rows[:, e * S : (e + 1) * S].reshape(
                        count * GY_N, CAP, S
                    )

        def message(q):
            return slots[q * GY_N : (q + 1) * GY_N].reshape(GY_N, MESSAGE, S).astype(BF16)

        nothing = jnp.zeros((GY_N, MESSAGE, S), BF16)

        @on_rod
        def _():
            collect(MEMB)
            send_a[0] = nothing
            send_b[0] = message(0)
            for q in range(1, PAIRS):
                send_a[q] = message(2 * q - 1)
                send_b[q] = message(2 * q)

        @on_membrane
        def _():
            collect(1)
            send_a[0] = message(0)
            send_b[0] = message(0)
            for q in range(1, PAIRS):
                send_a[q] = nothing
                send_b[q] = nothing

        copies.append(pltpu.make_async_copy(send_a, own_a_out, copied.at[1]))
        copies.append(pltpu.make_async_copy(send_b, own_b_out, copied.at[2]))
        for copy in copies[1:]:
            copy.start()
        for copy in copies:
            copy.wait()


def update(turn, scaled, args):
    first, last = turn == 0, turn == MATVECS
    if last:
        out = [jax.ShapeDtypeStruct((ROWS, S), F32)]
    else:
        out = [jax.ShapeDtypeStruct((NB, TILE, S), BF16)]
        out += [jax.ShapeDtypeStruct((TILE, S), BF16)] * 4
        out += [jax.ShapeDtypeStruct((PAIRS, GY_N, MESSAGE, S), BF16)] * 3
    if not first:
        out += [jax.ShapeDtypeStruct((1, S), F32)]
    if turn == 1:
        out += [jax.ShapeDtypeStruct((SLOTS, S), F32)]
    specs = [VMEM] * len(out)
    scratch = [pltpu.VMEM((MEMB * GY_N, DOFS, CAP, S), F32)]
    if not last:
        specs[0] = specs[6] = specs[7] = HBM
        scratch += [pltpu.VMEM((NB, TILE, S), BF16), pltpu.VMEM((PAIRS, GY_N, MESSAGE, S), BF16)]
        scratch += [pltpu.SemaphoreType.DMA((3,))]
    if not first and not last:
        scratch += [pltpu.VMEM((ROWS, S), F32)]
    return pl.pallas_call(
        functools.partial(update_kernel, turn, scaled),
        out_shape=out,
        in_specs=[SMEM] + [VMEM] * (len(args) - 1),
        out_specs=specs,
        scratch_shapes=scratch,
        compiler_params=pltpu.CompilerParams(vmem_limit_bytes=VMEM_BYTES),
        name="update",
    )(*args)


def inner_kernel(columns, blocks, rounded, out, token, extended, copied):
    copy = pltpu.make_async_copy(rounded, extended.at[:NB], copied)
    copy.start()
    extended[NB] = jnp.zeros((TILE, S), BF16)
    copy.wait()
    for r in range(NB):
        row = jnp.concatenate([blocks[r, k] for k in range(KB)], axis=1)
        picked = jnp.concatenate(
            [extended[jnp.minimum(columns[r, k], NB)] for k in range(KB)], axis=0
        )
        out[r * TILE : (r + 1) * TILE] = dot(row, picked)
    token[...] = out[:8]


def inner(columns, blocks, rounded):
    return pl.pallas_call(
        inner_kernel,
        out_shape=[jax.ShapeDtypeStruct((ROWS, S), F32), jax.ShapeDtypeStruct((8, S), F32)],
        in_specs=[SMEM, VMEM, HBM],
        out_specs=[VMEM, VMEM],
        scratch_shapes=[pltpu.VMEM((NB + 1, TILE, S), BF16), pltpu.SemaphoreType.DMA],
        compiler_params=pltpu.CompilerParams(vmem_limit_bytes=VMEM_BYTES),
        cost_estimate=pl.CostEstimate(
            flops=2 * NB * KB * TILE * TILE * S, bytes_accessed=12_000_000, transcendentals=0
        ),
        name="inner",
    )(columns, blocks, rounded)


def outer_kernel(columns, flags, blocks, base, x_even, x_odd, y_even, y_odd, out, edges, tiles, copied):
    terms = [(r, k) for r in range(NB) for k in range(1, KB)]
    copies = [
        pltpu.make_async_copy(blocks.at[r, k], tiles.at[j], copied.at[j])
        for j, (r, k) in enumerate(terms)
    ]
    for j, (r, k) in enumerate(terms):
        pl.when(columns[r, k] >= NB)(copies[j].start)
    odd_x, odd_y = flags[1], flags[2]
    edges[1 - odd_x] = x_even[...]
    edges[odd_x] = x_odd[...]
    edges[3 - odd_y] = y_even[...]
    edges[2 + odd_y] = y_odd[...]
    out[...] = base[...]
    for j, (r, k) in enumerate(terms):

        @pl.when(columns[r, k] >= NB)
        def _():
            copies[j].wait()
            out[r * TILE : (r + 1) * TILE] += dot(tiles[j], edges[columns[r, k] - NB])


def outer(columns, flags, blocks, base, halo):
    count = NB * (KB - 1)
    return pl.pallas_call(
        outer_kernel,
        out_shape=jax.ShapeDtypeStruct((ROWS, S), F32),
        in_specs=[SMEM, SMEM, HBM] + [VMEM] * 5,
        out_specs=VMEM,
        scratch_shapes=[
            pltpu.VMEM((4, TILE, S), BF16),
            pltpu.VMEM((count, TILE, TILE), BF16),
            pltpu.SemaphoreType.DMA((count,)),
        ],
        compiler_params=pltpu.CompilerParams(vmem_limit_bytes=VMEM_BYTES),
        cost_estimate=pl.CostEstimate(
            flops=8 * 2 * TILE * TILE * S, bytes_accessed=6_000_000, transcendentals=0
        ),
        name="outer",
    )(columns, flags, blocks, base, *halo)


def swaps(count, start):
    pairs = []
    for i in range(start, count - 1, 2):
        pairs += [(i, i + 1), (i + 1, i)]
    return pairs


def halos(edges):
    (x_even, x_odd, y_even, y_odd) = edges
    return (
        lax.ppermute(x_even, "gx", swaps(GX_N, 0)),
        lax.ppermute(x_odd, "gx", swaps(GX_N, 1)),
        lax.ppermute(y_even, GY, swaps(GY_N, 0)),
        lax.ppermute(y_odd, GY, swaps(GY_N, 1)),
    )


def total_of(rows):
    total = rows.reshape(1, -1)
    for axes, count in ((("gx", "y"), 16), (("zh", "core", "zl"), 16)):
        spread = jnp.broadcast_to(total, (count, total.shape[1]))
        gathered = lax.all_to_all(spread, axes, split_axis=0, concat_axis=0, tiled=True)
        total = jnp.sum(gathered, axis=0, keepdims=True)
    return total.reshape(rows.shape)


def merge_kernel(flags, own, passed, *refs):
    copied = refs[-1]
    out = refs[-2]
    group = flags[0]

    @pl.when(group == 0)
    def _():
        copy = pltpu.make_async_copy(own.at[1:], out.at[1:], copied)
        copy.start()
        out[0] = passed[0]
        copy.wait()

    @pl.when(group == 1)
    def _():
        out[...] = passed[...]

    @pl.when(group > 1)
    def _():
        copy = pltpu.make_async_copy(own.at[0], out.at[0], copied)
        copy.start()
        if len(refs) > 2:
            out[1] = refs[0][...]
        copy.wait()


def merge(flags, own, passed, extra):
    return pl.pallas_call(
        merge_kernel,
        out_shape=jax.ShapeDtypeStruct(own.shape, own.dtype),
        in_specs=[SMEM, HBM] + [VMEM] * (1 + len(extra)),
        out_specs=VMEM,
        scratch_shapes=[pltpu.SemaphoreType.DMA],
        compiler_params=pltpu.CompilerParams(vmem_limit_bytes=VMEM_BYTES),
        name="merge",
    )(flags, own, passed, *extra)


def exchange(send):
    return lax.all_to_all(
        send.reshape(PAIRS * GY_N, MESSAGE, S),
        ("zh", "y", "zl"),
        split_axis=0,
        concat_axis=0,
        tiled=True,
    ).reshape(PAIRS, GY_N, MESSAGE, S)


def after_kernel(value, *refs):
    refs[-1][...] = value[...]


def after(value, tokens):
    return pl.pallas_call(
        after_kernel,
        out_shape=jax.ShapeDtypeStruct(value.shape, value.dtype),
        in_specs=[VMEM] * (1 + len(tokens)),
        out_specs=VMEM,
        compiler_params=pltpu.CompilerParams(vmem_limit_bytes=VMEM_BYTES),
        name="after",
    )(value, *tokens)


def split(values):
    high = lax.reduce_precision(values, 8, 7)
    middle = lax.reduce_precision(values - high, 8, 7)
    return jnp.stack([high, middle, values - high - middle], axis=-1).astype(BF16)


def local(start_vectors, tile_blocks, block_columns, sleeve_rod, sleeve_membrane, sleeve_stiffness):
    group = lax.axis_index(GROUP)
    is_rod = group == 0
    memb = jnp.maximum(group - 1, 0)
    blocks = tile_blocks[0, 0, 0]
    columns = block_columns[0, 0, 0]
    odd_x = lax.axis_index("gx") % 2
    odd_y = lax.axis_index("zl")
    flags = jnp.stack([group, odd_x, odd_y])

    rod_nodes = sleeve_rod[0, 0].reshape(SLOTS)
    memb_nodes = lax.dynamic_index_in_dim(
        sleeve_membrane[0, :, :, 0, :], memb, axis=1, keepdims=False
    ).reshape(MSLOTS)
    rest = SLOTS - MSLOTS
    memb_nodes = jnp.concatenate([memb_nodes, jnp.full((rest,), -1, jnp.int32)])
    nodes = jnp.where(is_rod, rod_nodes, memb_nodes)
    ids = jnp.arange(NODES, dtype=jnp.int32)
    gather = (nodes[:, None] == ids[None, :]).astype(BF16)
    scatter = (ids[:, None] == nodes[None, :]).astype(BF16)

    stiff = sleeve_stiffness[0, :, :, 0, :]
    pieces = split(stiff)
    low = pieces[:, :DOFS].reshape(GY_N, MESSAGE, 3)
    high = jnp.pad(pieces[:, DOFS], ((0, 0), (0, MESSAGE - CAP), (0, 0)))
    stiff_message = jnp.pad(jnp.concatenate([low, high], axis=2), ((0, 0), (0, 0), (0, S - 6)))
    kappa = lax.dynamic_index_in_dim(stiff, memb, axis=1, keepdims=False).reshape(MSLOTS)
    kappa = jnp.concatenate([kappa, jnp.zeros((rest,), F32)])
    kappa = jnp.broadcast_to(kappa[:, None], (SLOTS, S))
    start = start_vectors[0, 0, 0].reshape(ROWS, S)

    def step(turn, state, kappa, inverse=None):
        (rounded, *edges, send_b, own_a, own_b) = state[:8]
        passed = lax.ppermute(send_b, GROUP, [(0, 1), (1, 0)])
        received = exchange(merge(flags, own_a, passed, [stiff_message] if turn == 1 else []))
        halo = halos(edges)
        (part, token) = inner(columns, blocks, rounded)
        received = after(received, [token, *halo])
        handed = lax.ppermute(received, GROUP, [(1, 0)])
        base = outer(columns, flags, blocks, part, halo)
        args = [flags, base, received, handed, own_a, own_b, kappa, scatter]
        if turn < MATVECS:
            args += [gather]
        if turn == 1:
            args += [lax.ppermute(received[1], GROUP, [(2, 0)])]
        if inverse is not None:
            args += [inverse]
        return update(turn, inverse is not None, args)

    def begin():
        return step(1, update(0, False, [flags, start, gather]), kappa)

    once = begin()
    twice = step(2, once, once[9])
    (value, last) = step(3, twice, once[9])

    sums = total_of(jnp.concatenate([once[8], twice[8], last], axis=0)) / ALL_DOFS
    safe = jnp.all((sums > LOWEST) & (sums < HIGHEST))
    first_norm = jnp.sqrt(sums[0:1] + EPS)

    def quick(_):
        second_norm = jnp.sqrt(sums[1:2] / jnp.square(first_norm) + EPS)
        both = first_norm * second_norm
        third_norm = jnp.sqrt(sums[2:3] / jnp.square(both) + EPS)
        final = value * (1.0 / (both * third_norm))
        return (final, jnp.concatenate([first_norm, second_norm, third_norm], axis=0))

    def careful(_):
        state = begin()
        kappa = state[9]
        state = step(2, state, kappa, 1.0 / first_norm)
        second_norm = jnp.sqrt(total_of(state[8]) / ALL_DOFS + EPS)
        (value, squares) = step(3, state, kappa, 1.0 / second_norm)
        third_norm = jnp.sqrt(total_of(squares) / ALL_DOFS + EPS)
        norms = jnp.concatenate([first_norm, second_norm, third_norm], axis=0)
        return (value / third_norm, norms)

    (final, norms) = lax.cond(safe, quick, careful, None)
    return (final.reshape(1, 1, 1, NB, TILE, S), norms)


def solution(mesh):
    fine = Mesh(mesh.devices.reshape(4, 2, GX_N, 4, 2), AXES)
    spread = (GROUP, "gx", GY)
    return jax.shard_map(
        local,
        mesh=fine,
        in_specs=(
            P(*spread, None, None, None),
            P(*spread, None, None, None, None),
            P(*spread, None, None),
            P("gx", GY, None, None, None),
            P("gx", None, None, GY, None),
            P("gx", None, None, GY, None),
        ),
        out_specs=(P(*spread, None, None, None), P()),
        check_vma=False,
    )
```

```python
import functools

import jax
import jax.numpy as jnp
from jax import lax
from jax.experimental import pallas as pl
from jax.experimental.pallas import tpu as pltpu
from jax.sharding import Mesh, PartitionSpec as P

MATVECS = 3
TILE = 384
NB = 8
KB = 4
S = 128
CAP = 8
DOFS = 6
NODES = NB * TILE // DOFS
ROWS = NB * TILE
GROUPS = 8
MEMB = GROUPS - 1
GX_N = 4
GY_N = 8
DEVICES = GROUPS * GX_N * GY_N
SLOTS = MEMB * GY_N * CAP
MSLOTS = GY_N * CAP
MESSAGE = DOFS * CAP
EPS = 1e-06
ALL_DOFS = DEVICES * ROWS
LOWEST, HIGHEST = 1e-20, 1e20

GROUP = ("zh", "core")
GY = ("y", "zl")
AXES = ("zh", "core", "gx", "y", "zl")
PAIRS = GROUPS // 2

VMEM = pl.BlockSpec(memory_space=pltpu.VMEM)
SMEM = pl.BlockSpec(memory_space=pltpu.SMEM)
HBM = pl.BlockSpec(memory_space=pltpu.HBM)
BF16 = jnp.bfloat16
F32 = jnp.float32
VMEM_BYTES = 20 * 1024 * 1024


def dot(a, b):
    return jnp.dot(a, b, preferred_element_type=F32)


def update_kernel(turn, scaled, *refs):
    refs = list(refs)
    take = lambda n: [refs.pop(0) for _ in range(n)]
    first, last = turn == 0, turn == MATVECS
    (flags, base) = take(2)
    if first:
        (gather,) = take(1)
    else:
        (received, handed, own_a, own_b, kappa_in, scatter) = take(6)
        if not last:
            (gather,) = take(1)
        if turn == 1:
            (stiff_message,) = take(1)
        if scaled:
            (inverse,) = take(1)
    if last:
        (y,) = take(1)
    else:
        (rounded_out, x_even, x_odd, y_even, y_odd, send_a, send_b, own_a_out, own_b_out) = take(9)
    if not first:
        (squares,) = take(1)
    kappa = None
    if turn == 1:
        (kappa,) = take(1)
    elif not first:
        kappa = kappa_in
    if scaled:
        (y,) = take(1)
    (slots,) = take(1)
    if not last:
        (rounded, copied) = take(2)
    if not first and not last and not scaled:
        (y,) = take(1)
    is_rod = flags[0] == 0

    def on_rod(f):
        pl.when(is_rod)(f)

    def on_membrane(f):
        pl.when(jnp.logical_not(is_rod))(f)

    if not first:

        def difference(q, mine, theirs):
            gap = mine[...].astype(F32) - theirs[...].astype(F32)
            stiff = kappa[q * MSLOTS : (q + 1) * MSLOTS].reshape(GY_N, 1, CAP, S)
            slots[q * GY_N : (q + 1) * GY_N] = gap.reshape(GY_N, DOFS, CAP, S) * stiff

        @on_rod
        def _():
            if turn == 1:
                parts = stiff_message[...].astype(F32)
                lane = lax.broadcasted_iota(jnp.int32, parts.shape, 2)
                low = jnp.sum(jnp.where(lane < 3, parts, 0.0), axis=2, keepdims=True)
                high = jnp.sum(
                    jnp.where((lane >= 3) & (lane < 6), parts, 0.0)[:, :CAP], axis=2, keepdims=True
                )
                for q in range(MEMB):
                    value = low[:, q * CAP : (q + 1) * CAP] if q < DOFS else high
                    kappa[q * MSLOTS : (q + 1) * MSLOTS] = jnp.broadcast_to(
                        value, (GY_N, CAP, S)
                    ).reshape(MSLOTS, S)
            difference(0, own_b.at[0], received.at[0])
            for q in range(1, PAIRS):
                difference(2 * q - 1, own_a.at[q], received.at[q])
                difference(2 * q, own_b.at[q], handed.at[q])

        @on_membrane
        def _():
            if turn == 1:
                kappa[...] = kappa_in[...]
            difference(0, own_a.at[0], received.at[0])
            slots[GY_N : 2 * GY_N] = jnp.zeros((GY_N, DOFS, CAP, S), F32)

        def pair_of(count, d):
            return jnp.concatenate(
                [slots[:count, d].reshape(count * CAP, S), slots[:count, d + 1].reshape(count * CAP, S)],
                axis=1,
            )

        def finish(d, coupling):
            value = base[pl.ds(d, NODES, stride=DOFS), :] + coupling
            if scaled:
                value = value * inverse[...]
            y[pl.ds(d, NODES, stride=DOFS), :] = value
            return jnp.sum(jnp.square(value).reshape(NODES // 8, 8, S), axis=0)

        @on_rod
        def _():
            total = jnp.zeros((8, S), F32)
            for d in range(0, DOFS, 2):
                coupling = dot(scatter[...], pair_of(MEMB * GY_N, d).astype(BF16))
                total += finish(d, coupling[:, :S]) + finish(d + 1, coupling[:, S:])
            squares[...] = jnp.sum(total, axis=0, keepdims=True)

        @on_membrane
        def _():
            total = jnp.zeros((8, S), F32)
            place = scatter[:, : 2 * MSLOTS]
            for d in range(0, DOFS, 2):
                delta = pair_of(2 * GY_N, d)
                high = delta.astype(BF16)
                low = (delta - high.astype(F32)).astype(BF16)
                coupling = dot(place, high) + dot(place, low)
                total += finish(d, coupling[:, :S]) + finish(d + 1, coupling[:, S:])
            squares[...] = jnp.sum(total, axis=0, keepdims=True)

    if not last:
        source = base if first else y

        for r in range(NB):
            rounded[r] = source[r * TILE : (r + 1) * TILE].astype(BF16)
        copies = [pltpu.make_async_copy(rounded, rounded_out, copied.at[0])]
        copies[0].start()
        odd_x, odd_y = flags[1], flags[2]
        x_even[...] = rounded[(NB - 1) * (1 - odd_x)]
        x_odd[...] = rounded[(NB - 1) * odd_x]
        y_even[...] = rounded[1 + (NB - 3) * odd_y]
        y_odd[...] = rounded[NB - 2 - (NB - 3) * odd_y]

        def collect(count):
            pick = gather[: count * MSLOTS]
            for d in range(0, DOFS, 2):
                values = jnp.concatenate(
                    [source[pl.ds(d + e, NODES, stride=DOFS), :].astype(BF16) for e in range(2)],
                    axis=1,
                )
                rows = dot(pick, values)
                for e in range(2):
                    slots[: count * GY_N, d + e] = rows[:, e * S : (e + 1) * S].reshape(
                        count * GY_N, CAP, S
                    )

        def message(q):
            return slots[q * GY_N : (q + 1) * GY_N].reshape(GY_N, MESSAGE, S).astype(BF16)

        nothing = jnp.zeros((GY_N, MESSAGE, S), BF16)

        @on_rod
        def _():
            collect(MEMB)
            send_a[0] = nothing
            send_b[0] = message(0)
            for q in range(1, PAIRS):
                send_a[q] = message(2 * q - 1)
                send_b[q] = message(2 * q)

        @on_membrane
        def _():
            collect(1)
            send_a[0] = message(0)
            send_b[0] = message(0)
            for q in range(1, PAIRS):
                send_a[q] = nothing
                send_b[q] = nothing

        copies.append(pltpu.make_async_copy(send_a, own_a_out, copied.at[1]))
        copies.append(pltpu.make_async_copy(send_b, own_b_out, copied.at[2]))
        for copy in copies[1:]:
            copy.start()
        for copy in copies:
            copy.wait()


def update(turn, scaled, args):
    first, last = turn == 0, turn == MATVECS
    if last:
        out = [jax.ShapeDtypeStruct((ROWS, S), F32)]
    else:
        out = [pltpu.HBM((NB, TILE, S), BF16)]
        out += [jax.ShapeDtypeStruct((TILE, S), BF16)] * 4
        out += [jax.ShapeDtypeStruct((PAIRS, GY_N, MESSAGE, S), BF16)] * 2
        out += [pltpu.HBM((PAIRS, GY_N, MESSAGE, S), BF16)] * 2
    if not first:
        out += [jax.ShapeDtypeStruct((1, S), F32)]
    if turn == 1:
        out += [jax.ShapeDtypeStruct((SLOTS, S), F32)]
    if scaled:
        out += [jax.ShapeDtypeStruct((ROWS, S), F32)]
    specs = [VMEM] * len(out)
    scratch = [pltpu.VMEM((MEMB * GY_N, DOFS, CAP, S), F32)]
    if not last:
        specs[0] = specs[7] = specs[8] = HBM
        scratch += [pltpu.VMEM((NB, TILE, S), BF16), pltpu.SemaphoreType.DMA((3,))]
    if not first and not last and not scaled:
        scratch += [pltpu.VMEM((ROWS, S), F32)]
    return pl.pallas_call(
        functools.partial(update_kernel, turn, scaled),
        out_shape=out,
        in_specs=[SMEM] + [VMEM] * (len(args) - 1),
        out_specs=specs,
        scratch_shapes=scratch,
        compiler_params=pltpu.CompilerParams(vmem_limit_bytes=VMEM_BYTES),
        name="update",
    )(*args)


def inner_kernel(columns, blocks, rounded, out, token, extended, copied):
    copy = pltpu.make_async_copy(rounded, extended.at[:NB], copied)
    copy.start()
    extended[NB] = jnp.zeros((TILE, S), BF16)
    copy.wait()

    def row_of(r, _):
        row = jnp.concatenate([blocks[r, k] for k in range(KB)], axis=1)
        picked = jnp.concatenate(
            [extended[jnp.minimum(columns[r, k], NB)] for k in range(KB)], axis=0
        )
        out[pl.ds(pl.multiple_of(r * TILE, TILE), TILE)] = dot(row, picked)
        return 0

    lax.fori_loop(0, NB, row_of, 0, unroll=4)
    token[...] = out[:8]


def inner(columns, blocks, rounded):
    return pl.pallas_call(
        inner_kernel,
        out_shape=[jax.ShapeDtypeStruct((ROWS, S), F32), jax.ShapeDtypeStruct((8, S), F32)],
        in_specs=[SMEM, VMEM, HBM],
        out_specs=[VMEM, VMEM],
        scratch_shapes=[pltpu.VMEM((NB + 1, TILE, S), BF16), pltpu.SemaphoreType.DMA],
        compiler_params=pltpu.CompilerParams(vmem_limit_bytes=VMEM_BYTES),
        cost_estimate=pl.CostEstimate(
            flops=2 * NB * KB * TILE * TILE * S, bytes_accessed=12_000_000, transcendentals=0
        ),
        name="inner",
    )(columns, blocks, rounded)


def outer_kernel(columns, flags, blocks, base, x_even, x_odd, y_even, y_odd, out, edges, tiles, copied):
    def copy_of(r, k):
        j = r * (KB - 1) + k - 1
        return pltpu.make_async_copy(blocks.at[r, k], tiles.at[j], copied.at[j])

    def fetch(r, _):
        for k in range(1, KB):
            pl.when(columns[r, k] >= NB)(copy_of(r, k).start)
        return 0

    lax.fori_loop(0, NB, fetch, 0)
    odd_x, odd_y = flags[1], flags[2]
    edges[1 - odd_x] = x_even[...]
    edges[odd_x] = x_odd[...]
    edges[3 - odd_y] = y_even[...]
    edges[2 + odd_y] = y_odd[...]

    def add(r, _):
        rows = pl.ds(pl.multiple_of(r * TILE, TILE), TILE)
        out[rows] = base[rows]
        for k in range(1, KB):

            @pl.when(columns[r, k] >= NB)
            def _():
                copy_of(r, k).wait()
                out[rows] += dot(tiles[r * (KB - 1) + k - 1], edges[columns[r, k] - NB])

        return 0

    lax.fori_loop(0, NB, add, 0)


def outer(columns, flags, blocks, base, halo):
    count = NB * (KB - 1)
    return pl.pallas_call(
        outer_kernel,
        out_shape=jax.ShapeDtypeStruct((ROWS, S), F32),
        in_specs=[SMEM, SMEM, HBM] + [VMEM] * 5,
        out_specs=VMEM,
        scratch_shapes=[
            pltpu.VMEM((4, TILE, S), BF16),
            pltpu.VMEM((count, TILE, TILE), BF16),
            pltpu.SemaphoreType.DMA((count,)),
        ],
        compiler_params=pltpu.CompilerParams(vmem_limit_bytes=VMEM_BYTES),
        cost_estimate=pl.CostEstimate(
            flops=8 * 2 * TILE * TILE * S, bytes_accessed=6_000_000, transcendentals=0
        ),
        name="outer",
    )(columns, flags, blocks, base, *halo)


def swaps(count, start):
    pairs = []
    for i in range(start, count - 1, 2):
        pairs += [(i, i + 1), (i + 1, i)]
    return pairs


def halos(edges):
    (x_even, x_odd, y_even, y_odd) = edges
    return (
        lax.ppermute(x_even, "gx", swaps(GX_N, 0)),
        lax.ppermute(x_odd, "gx", swaps(GX_N, 1)),
        lax.ppermute(y_even, GY, swaps(GY_N, 0)),
        lax.ppermute(y_odd, GY, swaps(GY_N, 1)),
    )


def total_of(rows):
    total = rows.reshape(1, -1)
    for axes, count in ((("gx", "y"), 16), (("zh", "core", "zl"), 16)):
        spread = jnp.broadcast_to(total, (count, total.shape[1]))
        gathered = lax.all_to_all(spread, axes, split_axis=0, concat_axis=0, tiled=True)
        total = jnp.sum(gathered, axis=0, keepdims=True)
    return total.reshape(rows.shape)


def merge(group, own, passed, extra):
    block = jnp.arange(PAIRS)
    relay = (group == 1) | ((group == 0) & (block == 0))
    send = jnp.where(relay[:, None, None, None], passed, own)
    if extra is not None:
        free = (group > 1) & (block == 1)
        send = jnp.where(free[:, None, None, None], extra[None], send)
    return send


def exchange(send):
    return lax.all_to_all(
        send.reshape(PAIRS * GY_N, MESSAGE, S),
        ("zh", "y", "zl"),
        split_axis=0,
        concat_axis=0,
        tiled=True,
    ).reshape(PAIRS, GY_N, MESSAGE, S)


def after_kernel(value, *refs):
    refs[-1][...] = value[...]


def after(value, tokens):
    return pl.pallas_call(
        after_kernel,
        out_shape=jax.ShapeDtypeStruct(value.shape, value.dtype),
        in_specs=[VMEM] * (1 + len(tokens)),
        out_specs=VMEM,
        compiler_params=pltpu.CompilerParams(vmem_limit_bytes=VMEM_BYTES),
        name="after",
    )(value, *tokens)


def split(values):
    high = lax.reduce_precision(values, 8, 7)
    middle = lax.reduce_precision(values - high, 8, 7)
    return jnp.stack([high, middle, values - high - middle], axis=-1).astype(BF16)


def local(start_vectors, tile_blocks, block_columns, sleeve_rod, sleeve_membrane, sleeve_stiffness):
    group = lax.axis_index(GROUP)
    is_rod = group == 0
    memb = jnp.maximum(group - 1, 0)
    blocks = tile_blocks[0, 0, 0]
    columns = block_columns[0, 0, 0]
    odd_x = lax.axis_index("gx") % 2
    odd_y = lax.axis_index("zl")
    flags = jnp.stack([group, odd_x, odd_y])

    rod_nodes = sleeve_rod[0, 0].reshape(SLOTS)
    memb_nodes = lax.dynamic_index_in_dim(
        sleeve_membrane[0, :, :, 0, :], memb, axis=1, keepdims=False
    ).reshape(MSLOTS)
    rest = SLOTS - MSLOTS
    memb_nodes = jnp.concatenate([memb_nodes, jnp.full((rest,), -1, jnp.int32)])
    nodes = jnp.where(is_rod, rod_nodes, memb_nodes)
    ids = jnp.arange(NODES, dtype=jnp.int32)
    gather = (nodes[:, None] == ids[None, :]).astype(BF16)
    scatter = (ids[:, None] == nodes[None, :]).astype(BF16)

    stiff = sleeve_stiffness[0, :, :, 0, :]
    pieces = split(stiff)
    low = pieces[:, :DOFS].reshape(GY_N, MESSAGE, 3)
    high = jnp.pad(pieces[:, DOFS], ((0, 0), (0, MESSAGE - CAP), (0, 0)))
    stiff_message = jnp.pad(jnp.concatenate([low, high], axis=2), ((0, 0), (0, 0), (0, S - 6)))
    kappa = lax.dynamic_index_in_dim(stiff, memb, axis=1, keepdims=False).reshape(MSLOTS)
    kappa = jnp.concatenate([kappa, jnp.zeros((rest,), F32)])
    kappa = jnp.broadcast_to(kappa[:, None], (SLOTS, S))
    start = start_vectors[0, 0, 0].reshape(ROWS, S)

    def step(turn, state, kappa, inverse=None):
        (rounded, *edges, send_a, send_b, own_a, own_b) = state[:9]
        passed = lax.ppermute(send_b, GROUP, [(0, 1), (1, 0)])
        received = exchange(merge(group, send_a, passed, stiff_message if turn == 1 else None))
        halo = halos(edges)
        (part, token) = inner(columns, blocks, rounded)
        received = after(received, [token, *halo])
        handed = lax.ppermute(received, GROUP, [(1, 0)])
        base = outer(columns, flags, blocks, part, halo)
        args = [flags, base, received, handed, own_a, own_b, kappa, scatter]
        if turn < MATVECS:
            args += [gather]
        if turn == 1:
            args += [lax.ppermute(received[1], GROUP, [(2, 0)])]
        if inverse is not None:
            args += [inverse]
        return update(turn, inverse is not None, args)

    begun = update(0, False, [flags, start, gather])
    once = step(1, begun, kappa)
    kappa = once[10]
    twice = step(2, once, kappa)
    (value, last) = step(3, twice, kappa)

    sums = total_of(jnp.concatenate([once[9], twice[9], last], axis=0)) / ALL_DOFS
    safe = jnp.all((sums > LOWEST) & (sums < HIGHEST))
    first_norm = jnp.sqrt(sums[0:1] + EPS)

    def quick(_):
        second_norm = jnp.sqrt(sums[1:2] / jnp.square(first_norm) + EPS)
        both = first_norm * second_norm
        third_norm = jnp.sqrt(sums[2:3] / jnp.square(both) + EPS)
        final = value * (1.0 / (both * third_norm))
        return (final, jnp.concatenate([first_norm, second_norm, third_norm], axis=0))

    def careful(_):
        def turn(k, carry):
            (state, norm, norms, _) = carry
            (*state, squares, value) = step(2, state, kappa, 1.0 / norm)
            norm = jnp.sqrt(total_of(squares) / ALL_DOFS + EPS)
            return (state, norm, norms.at[k].set(norm[0]), value)

        state = update(0, False, [flags, start, gather])
        zero = jnp.zeros((MATVECS, S), F32)
        carry = (list(state), jnp.ones((1, S), F32), zero, jnp.zeros((ROWS, S), F32))
        (_, norm, norms, value) = lax.fori_loop(0, MATVECS, turn, carry)
        return (value / norm, norms)

    (final, norms) = lax.cond(safe, quick, careful, None)
    return (final.reshape(1, 1, 1, NB, TILE, S), norms)


def solution(mesh):
    fine = Mesh(mesh.devices.reshape(4, 2, GX_N, 4, 2), AXES)
    spread = (GROUP, "gx", GY)
    return jax.shard_map(
        local,
        mesh=fine,
        in_specs=(
            P(*spread, None, None, None),
            P(*spread, None, None, None, None),
            P(*spread, None, None),
            P("gx", GY, None, None, None),
            P("gx", None, None, GY, None),
            P("gx", None, None, GY, None),
        ),
        out_specs=(P(*spread, None, None, None), P()),
        check_vma=False,
    )
```

```python
import functools

import jax
import jax.numpy as jnp
from jax import lax
from jax.experimental import pallas as pl
from jax.experimental.pallas import tpu as pltpu
from jax.sharding import Mesh, PartitionSpec as P

MATVECS = 3
TILE = 384
NB = 8
KB = 4
NEAR = NB + 2
S = 128
CAP = 8
DOFS = 6
NODES = NB * TILE // DOFS
ROWS = NB * TILE
GROUPS = 8
MEMB = GROUPS - 1
GX_N = 4
GY_N = 8
DEVICES = GROUPS * GX_N * GY_N
SLOTS = MEMB * GY_N * CAP
MSLOTS = GY_N * CAP
MESSAGE = DOFS * CAP
EPS = 1e-06
ALL_DOFS = DEVICES * ROWS
LOWEST, HIGHEST = 1e-20, 1e20

GROUP = ("zh", "core")
GY = ("y", "zl")
AXES = ("zh", "core", "gx", "y", "zl")
PAIRS = GROUPS // 2

VMEM = pl.BlockSpec(memory_space=pltpu.VMEM)
SMEM = pl.BlockSpec(memory_space=pltpu.SMEM)
HBM = pl.BlockSpec(memory_space=pltpu.HBM)
BF16 = jnp.bfloat16
F32 = jnp.float32
VMEM_BYTES = 20 * 1024 * 1024


def dot(a, b):
    return jnp.dot(a, b, preferred_element_type=F32)


def update_kernel(turn, scaled, *refs):
    refs = list(refs)
    take = lambda n: [refs.pop(0) for _ in range(n)]
    first, last = turn == 0, turn == MATVECS
    (flags, base) = take(2)
    if first:
        (gather,) = take(1)
    else:
        (received, handed, own_a, own_b, kappa_in, scatter) = take(6)
        if not last:
            (gather,) = take(1)
        if turn == 1:
            (stiff_message,) = take(1)
        if scaled:
            (inverse,) = take(1)
    if last:
        (y,) = take(1)
    else:
        (rounded_out, x_even, x_odd, y_even, y_odd, send_a, send_b, own_a_out, own_b_out) = take(9)
    if not first:
        (squares,) = take(1)
    kappa = None
    if turn == 1:
        (kappa,) = take(1)
    elif not first:
        kappa = kappa_in
    if scaled:
        (y,) = take(1)
    (slots,) = take(1)
    if not last:
        (rounded, copied) = take(2)
    if not first and not last and not scaled:
        (y,) = take(1)
    is_rod = flags[0] == 0

    def on_rod(f):
        pl.when(is_rod)(f)

    def on_membrane(f):
        pl.when(jnp.logical_not(is_rod))(f)

    if not first:

        def difference(q, mine, theirs):
            gap = mine[...].astype(F32) - theirs[...].astype(F32)
            stiff = kappa[q * MSLOTS : (q + 1) * MSLOTS].reshape(GY_N, 1, CAP, S)
            slots[q * GY_N : (q + 1) * GY_N] = gap.reshape(GY_N, DOFS, CAP, S) * stiff

        @on_rod
        def _():
            if turn == 1:
                parts = stiff_message[...].astype(F32)
                lane = lax.broadcasted_iota(jnp.int32, parts.shape, 2)
                low = jnp.sum(jnp.where(lane < 3, parts, 0.0), axis=2, keepdims=True)
                high = jnp.sum(
                    jnp.where((lane >= 3) & (lane < 6), parts, 0.0)[:, :CAP], axis=2, keepdims=True
                )
                for q in range(MEMB):
                    value = low[:, q * CAP : (q + 1) * CAP] if q < DOFS else high
                    kappa[q * MSLOTS : (q + 1) * MSLOTS] = jnp.broadcast_to(
                        value, (GY_N, CAP, S)
                    ).reshape(MSLOTS, S)
            difference(0, own_b.at[0], received.at[0])
            for q in range(1, PAIRS):
                difference(2 * q - 1, own_a.at[q], received.at[q])
                difference(2 * q, own_b.at[q], handed.at[q])

        @on_membrane
        def _():
            if turn == 1:
                kappa[...] = kappa_in[...]
            difference(0, own_b.at[0], received.at[0])
            slots[GY_N : 2 * GY_N] = jnp.zeros((GY_N, DOFS, CAP, S), F32)

        def pair_of(count, d):
            return jnp.concatenate(
                [slots[:count, d].reshape(count * CAP, S), slots[:count, d + 1].reshape(count * CAP, S)],
                axis=1,
            )

        def finish(d, coupling):
            value = base[pl.ds(d, NODES, stride=DOFS), :] + coupling
            if scaled:
                value = value * inverse[...]
            y[pl.ds(d, NODES, stride=DOFS), :] = value
            return jnp.sum(jnp.square(value).reshape(NODES // 8, 8, S), axis=0)

        def couple(coupling_of):
            total = jnp.zeros((8, S), F32)
            for d in range(0, DOFS, 2):
                coupling = coupling_of(d)
                total += finish(d, coupling[:, :S]) + finish(d + 1, coupling[:, S:])
            squares[...] = jnp.sum(total, axis=0, keepdims=True)

        @on_rod
        def _():
            couple(lambda d: dot(scatter[...], pair_of(MEMB * GY_N, d).astype(BF16)))

        @on_membrane
        def _():
            place = scatter[:, : 2 * MSLOTS]

            def coupling_of(d):
                delta = pair_of(2 * GY_N, d)
                high = delta.astype(BF16)
                low = (delta - high.astype(F32)).astype(BF16)
                return dot(place, high) + dot(place, low)

            couple(coupling_of)

    if not last:
        source = base if first else y

        for r in range(NB):
            rounded[r] = source[r * TILE : (r + 1) * TILE].astype(BF16)
        copies = [pltpu.make_async_copy(rounded, rounded_out, copied.at[0])]
        copies[0].start()
        odd_x, odd_y = flags[1], flags[2]
        x_even[...] = rounded[(NB - 1) * (1 - odd_x)]
        x_odd[...] = rounded[(NB - 1) * odd_x]
        y_even[...] = rounded[1 + (NB - 3) * odd_y]
        y_odd[...] = rounded[NB - 2 - (NB - 3) * odd_y]

        def collect(count, put):
            pick = gather[: count * MSLOTS]
            for d in range(0, DOFS, 2):
                values = jnp.concatenate(
                    [source[pl.ds(d + e, NODES, stride=DOFS), :].astype(BF16) for e in range(2)],
                    axis=1,
                )
                found = dot(pick, values)
                both = [
                    found[:, e * S : (e + 1) * S].reshape(count * GY_N, 1, CAP, S) for e in range(2)
                ]
                rows = jnp.concatenate(both, axis=1).reshape(count * GY_N, 2 * CAP, S).astype(BF16)
                for q in range(count):
                    put(q, d, rows[q * GY_N : (q + 1) * GY_N])

        nothing = jnp.zeros((GY_N, MESSAGE, S), BF16)

        @on_rod
        def _():
            def put(q, d, rows):
                target = send_a if q % 2 else send_b
                target[(q + 1) // 2, :, d * CAP : (d + 2) * CAP] = rows

            collect(MEMB, put)
            send_a[0] = nothing

        @on_membrane
        def _():
            def put(q, d, rows):
                send_a[0, :, d * CAP : (d + 2) * CAP] = rows
                send_b[0, :, d * CAP : (d + 2) * CAP] = rows

            collect(1, put)
            for q in range(1, PAIRS):
                send_a[q] = nothing
                send_b[q] = nothing

        copies.append(pltpu.make_async_copy(send_a, own_a_out, copied.at[1]))
        copies.append(pltpu.make_async_copy(send_b, own_b_out, copied.at[2]))
        for copy in copies[1:]:
            copy.start()
        for copy in copies:
            copy.wait()


def update(turn, scaled, args):
    first, last = turn == 0, turn == MATVECS
    if last:
        out = [jax.ShapeDtypeStruct((ROWS, S), F32)]
    else:
        out = [pltpu.HBM((NB, TILE, S), BF16)]
        out += [jax.ShapeDtypeStruct((TILE, S), BF16)] * 4
        out += [jax.ShapeDtypeStruct((PAIRS, GY_N, MESSAGE, S), BF16)] * 2
        out += [pltpu.HBM((PAIRS, GY_N, MESSAGE, S), BF16)] * 2
    if not first:
        out += [jax.ShapeDtypeStruct((1, S), F32)]
    if turn == 1:
        out += [jax.ShapeDtypeStruct((SLOTS, S), F32)]
    if scaled:
        out += [jax.ShapeDtypeStruct((ROWS, S), F32)]
    specs = [VMEM] * len(out)
    scratch = [pltpu.VMEM((MEMB * GY_N, DOFS, CAP, S), F32)]
    if not last:
        specs[0] = specs[7] = specs[8] = HBM
        scratch += [pltpu.VMEM((NB, TILE, S), BF16), pltpu.SemaphoreType.DMA((3,))]
    if not first and not last and not scaled:
        scratch += [pltpu.VMEM((ROWS, S), F32)]
    return pl.pallas_call(
        functools.partial(update_kernel, turn, scaled),
        out_shape=out,
        in_specs=[SMEM] + [VMEM] * (len(args) - 1),
        out_specs=specs,
        scratch_shapes=scratch,
        compiler_params=pltpu.CompilerParams(vmem_limit_bytes=VMEM_BYTES),
        name="update",
    )(*args)


def inner_kernel(columns, flags, blocks, rounded, x_even, x_odd, *refs):
    (out, token, extended, tiles, copied) = refs
    half = NB // 2
    copies = [pltpu.make_async_copy(rounded, extended.at[:NB], copied.at[2])]
    for part in range(2):
        rows = pl.ds(part * half, half)
        copies.append(pltpu.make_async_copy(blocks.at[rows], tiles.at[rows], copied.at[part]))
    for copy in copies:
        copy.start()
    odd_x = flags[1]
    extended[NB + 1 - odd_x] = x_even[...]
    extended[NB + odd_x] = x_odd[...]
    extended[NEAR] = jnp.zeros((TILE, S), BF16)
    copies[0].wait()

    def row_of(r, _):
        row = jnp.concatenate([tiles[r, k] for k in range(KB)], axis=1)
        picked = jnp.concatenate(
            [extended[jnp.minimum(columns[r, k], NEAR)] for k in range(KB)], axis=0
        )
        out[pl.ds(pl.multiple_of(r * TILE, TILE), TILE)] = dot(row, picked)
        return 0

    for part in range(2):
        copies[part + 1].wait()
        lax.fori_loop(part * half, (part + 1) * half, row_of, 0, unroll=2)
    token[...] = out[:8]


def inner(columns, flags, blocks, rounded, x_even, x_odd):
    return pl.pallas_call(
        inner_kernel,
        out_shape=[jax.ShapeDtypeStruct((ROWS, S), F32), jax.ShapeDtypeStruct((8, S), F32)],
        in_specs=[SMEM, SMEM, HBM, HBM, VMEM, VMEM],
        out_specs=[VMEM, VMEM],
        scratch_shapes=[
            pltpu.VMEM((NEAR + 1, TILE, S), BF16),
            pltpu.VMEM((NB, KB, TILE, TILE), BF16),
            pltpu.SemaphoreType.DMA((3,)),
        ],
        compiler_params=pltpu.CompilerParams(vmem_limit_bytes=VMEM_BYTES),
        cost_estimate=pl.CostEstimate(
            flops=2 * NB * KB * TILE * TILE * S, bytes_accessed=12_000_000, transcendentals=0
        ),
        name="inner",
    )(columns, flags, blocks, rounded, x_even, x_odd)


def outer_kernel(columns, flags, blocks, base, y_even, y_odd, out, edges, tiles, copied):
    def copy_of(r, k):
        j = r * (KB - 1) + k - 1
        return pltpu.make_async_copy(blocks.at[r, k], tiles.at[j], copied.at[j])

    def fetch(r, _):
        for k in range(1, KB):
            pl.when(columns[r, k] >= NEAR)(copy_of(r, k).start)
        return 0

    lax.fori_loop(0, NB, fetch, 0)
    odd_y = flags[2]
    edges[1 - odd_y] = y_even[...]
    edges[odd_y] = y_odd[...]

    def add(r, _):
        rows = pl.ds(pl.multiple_of(r * TILE, TILE), TILE)
        out[rows] = base[rows]
        for k in range(1, KB):

            @pl.when(columns[r, k] >= NEAR)
            def _():
                copy_of(r, k).wait()
                out[rows] += dot(tiles[r * (KB - 1) + k - 1], edges[columns[r, k] - NEAR])

        return 0

    lax.fori_loop(0, NB, add, 0)


def outer(columns, flags, blocks, base, y_even, y_odd):
    count = NB * (KB - 1)
    return pl.pallas_call(
        outer_kernel,
        out_shape=jax.ShapeDtypeStruct((ROWS, S), F32),
        in_specs=[SMEM, SMEM, HBM] + [VMEM] * 3,
        out_specs=VMEM,
        scratch_shapes=[
            pltpu.VMEM((2, TILE, S), BF16),
            pltpu.VMEM((count, TILE, TILE), BF16),
            pltpu.SemaphoreType.DMA((count,)),
        ],
        compiler_params=pltpu.CompilerParams(vmem_limit_bytes=VMEM_BYTES),
        cost_estimate=pl.CostEstimate(
            flops=4 * 2 * TILE * TILE * S, bytes_accessed=6_000_000, transcendentals=0
        ),
        name="outer",
    )(columns, flags, blocks, base, y_even, y_odd)


def swaps(count, start):
    pairs = []
    for i in range(start, count - 1, 2):
        pairs += [(i, i + 1), (i + 1, i)]
    return pairs


def halos(edges):
    (x_even, x_odd, y_even, y_odd) = edges
    return (
        lax.ppermute(x_even, "gx", swaps(GX_N, 0)),
        lax.ppermute(x_odd, "gx", swaps(GX_N, 1)),
        lax.ppermute(y_even, GY, swaps(GY_N, 0)),
        lax.ppermute(y_odd, GY, swaps(GY_N, 1)),
    )


def total_of(rows):
    total = rows.reshape(1, -1)
    for axes, count in ((("gx", "y"), 16), (("zh", "core", "zl"), 16)):
        spread = jnp.broadcast_to(total, (count, total.shape[1]))
        gathered = lax.all_to_all(spread, axes, split_axis=0, concat_axis=0, tiled=True)
        total = jnp.sum(gathered, axis=0, keepdims=True)
    return total.reshape(rows.shape)


def merge(group, own, passed, extra):
    block = jnp.arange(PAIRS)
    relay = (group == 1) | ((group == 0) & (block == 0))
    send = jnp.where(relay[:, None, None, None], passed, own)
    if extra is not None:
        free = (group > 1) & (block == 1)
        send = jnp.where(free[:, None, None, None], extra[None], send)
    return send


def exchange(send):
    return lax.all_to_all(
        send.reshape(PAIRS * GY_N, MESSAGE, S),
        ("zh", "y", "zl"),
        split_axis=0,
        concat_axis=0,
        tiled=True,
    ).reshape(PAIRS, GY_N, MESSAGE, S)


def after_kernel(value, *refs):
    refs[-1][...] = value[...]


def after(value, tokens):
    return pl.pallas_call(
        after_kernel,
        out_shape=jax.ShapeDtypeStruct(value.shape, value.dtype),
        in_specs=[VMEM] * (1 + len(tokens)),
        out_specs=VMEM,
        compiler_params=pltpu.CompilerParams(vmem_limit_bytes=VMEM_BYTES),
        name="after",
    )(value, *tokens)


def split(values):
    high = lax.reduce_precision(values, 8, 7)
    middle = lax.reduce_precision(values - high, 8, 7)
    return jnp.stack([high, middle, values - high - middle], axis=-1).astype(BF16)


def local(start_vectors, tile_blocks, block_columns, sleeve_rod, sleeve_membrane, sleeve_stiffness):
    group = lax.axis_index(GROUP)
    is_rod = group == 0
    memb = jnp.maximum(group - 1, 0)
    blocks = tile_blocks[0, 0, 0]
    columns = block_columns[0, 0, 0]
    odd_x = lax.axis_index("gx") % 2
    odd_y = lax.axis_index("zl")
    flags = jnp.stack([group, odd_x, odd_y])

    rod_nodes = sleeve_rod[0, 0].reshape(SLOTS)
    memb_nodes = lax.dynamic_index_in_dim(
        sleeve_membrane[0, :, :, 0, :], memb, axis=1, keepdims=False
    ).reshape(MSLOTS)
    rest = SLOTS - MSLOTS
    memb_nodes = jnp.concatenate([memb_nodes, jnp.full((rest,), -1, jnp.int32)])
    nodes = jnp.where(is_rod, rod_nodes, memb_nodes)
    ids = jnp.arange(NODES, dtype=jnp.int32)
    gather = (nodes[:, None] == ids[None, :]).astype(BF16)
    scatter = (ids[:, None] == nodes[None, :]).astype(BF16)

    stiff = sleeve_stiffness[0, :, :, 0, :]
    pieces = split(stiff)
    low = pieces[:, :DOFS].reshape(GY_N, MESSAGE, 3)
    high = jnp.pad(pieces[:, DOFS], ((0, 0), (0, MESSAGE - CAP), (0, 0)))
    stiff_message = jnp.pad(jnp.concatenate([low, high], axis=2), ((0, 0), (0, 0), (0, S - 6)))
    kappa = lax.dynamic_index_in_dim(stiff, memb, axis=1, keepdims=False).reshape(MSLOTS)
    kappa = jnp.concatenate([kappa, jnp.zeros((rest,), F32)])
    kappa = jnp.broadcast_to(kappa[:, None], (SLOTS, S))
    start = start_vectors[0, 0, 0].reshape(ROWS, S)

    def step(turn, state, kappa, inverse=None):
        (rounded, *edges, send_a, send_b, own_a, own_b) = state[:9]
        passed = lax.ppermute(send_b, GROUP, [(0, 1), (1, 0)])
        received = exchange(merge(group, send_a, passed, stiff_message if turn == 1 else None))
        (x_even, x_odd, y_even, y_odd) = halos(edges)
        (part, token) = inner(columns, flags, blocks, rounded, x_even, x_odd)
        received = after(received, [token, y_even, y_odd])
        handed = lax.ppermute(received, GROUP, [(1, 0)])
        base = outer(columns, flags, blocks, part, y_even, y_odd)
        args = [flags, base, received, handed, own_a, own_b, kappa, scatter]
        if turn < MATVECS:
            args += [gather]
        if turn == 1:
            args += [lax.ppermute(received[1], GROUP, [(2, 0)])]
        if inverse is not None:
            args += [inverse]
        return update(turn, inverse is not None, args)

    begun = update(0, False, [flags, start, gather])
    once = step(1, begun, kappa)
    kappa = once[10]
    twice = step(2, once, kappa)
    (value, last) = step(3, twice, kappa)

    sums = total_of(jnp.concatenate([once[9], twice[9], last], axis=0)) / ALL_DOFS
    safe = jnp.all((sums > LOWEST) & (sums < HIGHEST))
    first_norm = jnp.sqrt(sums[0:1] + EPS)

    def quick(_):
        second_norm = jnp.sqrt(sums[1:2] / jnp.square(first_norm) + EPS)
        both = first_norm * second_norm
        third_norm = jnp.sqrt(sums[2:3] / jnp.square(both) + EPS)
        final = value * (1.0 / (both * third_norm))
        return (final, jnp.concatenate([first_norm, second_norm, third_norm], axis=0))

    def careful(_):
        def turn(k, carry):
            (state, norm, norms, _) = carry
            (*state, squares, value) = step(2, state, kappa, 1.0 / norm)
            norm = jnp.sqrt(total_of(squares) / ALL_DOFS + EPS)
            return (state, norm, norms.at[k].set(norm[0]), value)

        state = update(0, False, [flags, start, gather])
        zero = jnp.zeros((MATVECS, S), F32)
        carry = (list(state), jnp.ones((1, S), F32), zero, jnp.zeros((ROWS, S), F32))
        (_, norm, norms, value) = lax.fori_loop(0, MATVECS, turn, carry)
        return (value / norm, norms)

    (final, norms) = lax.cond(safe, quick, careful, None)
    return (final.reshape(1, 1, 1, NB, TILE, S), norms)


def solution(mesh):
    fine = Mesh(mesh.devices.reshape(4, 2, GX_N, 4, 2), AXES)
    spread = (GROUP, "gx", GY)
    return jax.shard_map(
        local,
        mesh=fine,
        in_specs=(
            P(*spread, None, None, None),
            P(*spread, None, None, None, None),
            P(*spread, None, None),
            P("gx", GY, None, None, None),
            P("gx", None, None, GY, None),
            P("gx", None, None, GY, None),
        ),
        out_specs=(P(*spread, None, None, None), P()),
        check_vma=False,
    )
```
